512 devices in a mesh: segment: 4 (over x), cells: 128 (over z, y, core).
Axes of the slice: x: 4, y: 4, z: 16, core: 2. Of those that a mesh axis runs over, the one named last changes fastest.
Arguments:
- feats: bfloat16 [1, 32768, 256], P(None, 'cells'), may hold values from -6 to 6
- weights: bfloat16 [4, 256, 256], P('segment'), may hold values from -0.375 to 0.375
- gains: float32 [4, 256], P('segment'), may hold values from 0.25 to 1.75
- send_rows: int32 [1, 128, 128, 2], P(None, 'cells'), may hold values from 0 to 255, as said below
- send_count: int32 [1, 128, 128], P(None, 'cells'), may hold values from 1 to 2, as said below
- local_index: int32 [1, 128, 4, 2], P(None, 'cells'), may hold values from 0 to 1, as said below
- halo_index: int32 [1, 128, 2, 2], P(None, 'cells'), may hold values from 0 to 3, as said below
- block_count: int32 [1, 128, 2], P(None, 'cells'), may hold values from 1 to 4, as said below
- local_vals: bfloat16 [1, 512, 128, 128], P(None, 'cells'), may hold values from -0.3125 to 0.3125
- halo_vals: bfloat16 [1, 256, 128, 128], P(None, 'cells'), may hold values from -0.3125 to 0.3125
- cotangent: bfloat16 [1, 32768, 256], P(None, 'cells'), may hold values from -6 to 6
Outputs:
- layer_outputs: bfloat16 [4, 1, 32768, 256], P('segment', None, 'cells')
- input_grads: bfloat16 [4, 1, 32768, 256], P('segment', None, 'cells')
- weight_grads: float32 [4, 256, 256], P('segment')
- gain_grads: float32 [4, 256], P('segment')
The draws below stay inside these ranges and needn't reach their ends.
Inputs may be any that keep to these rules, and one draw needn't show every extreme that they name: `send_rows`: local row indices of the sender. `send_count`: in every slab, every sender fills all slots to some owner, and some owner is filled by every sender. `local_index`: row blocks and column blocks of the owner's own cells. `halo_index`: row blocks of own cells, and column blocks 2 and on for received rows. `block_count`: column 0 counts own blocks, at most 4; column 1 counts received blocks, at most 2; in every slab for each kind some owner has every block of that kind live.
All inputs are finite; a program needn't handle non-finite values.
Results may differ from the reference program's by a relative error of at most 0.015.
Values may be sent and summed in bfloat16 or wider, within the bound.
A program may use at most 64 MiB of HBM per device.

```python
import math
import jax
import jax.numpy as jnp
from jax import lax

D = 256
BLK = 128
MICRO = 1
ROW_BLOCKS = 2
HALO_ROWS = 256
LAYERS = 4
ROWS_DEV = 256
TOTAL_ROWS = 32768
PEER_SLOTS = 2
HALO_COLS = 2
LOCAL_BLOCKS = 4
HALO_BLOCKS = 2
N_CELLS = 128


def draw_send_rows(key, part):
    key = jax.random.fold_in(key, 11)
    return jax.random.randint(key, (MICRO, N_CELLS, N_CELLS, PEER_SLOTS), 0, ROWS_DEV, dtype=jnp.int32)


def count_one_slab(key):
    first, second, third = jax.random.split(key, 3)
    counts = jax.random.randint(first, (N_CELLS, N_CELLS), max(1, PEER_SLOTS // 2), PEER_SLOTS + 1, dtype=jnp.int32)
    chosen = jax.random.randint(second, (N_CELLS,), 0, N_CELLS, dtype=jnp.int32)
    counts = counts.at[jnp.arange(N_CELLS), chosen].set(PEER_SLOTS)
    owner = jax.random.randint(third, (), 0, N_CELLS, dtype=jnp.int32)
    filled = jnp.where(jnp.arange(N_CELLS)[None, :] == owner, PEER_SLOTS, counts)
    return filled.astype(jnp.int32)


def draw_send_count(key, part):
    key = jax.random.fold_in(key, 12)
    return jax.vmap(count_one_slab)(jax.random.split(key, MICRO)).astype(jnp.int32)


def draw_local_index(key, part):
    key = jax.random.fold_in(key, 13)
    first, second = jax.random.split(key)
    rowblk = jax.random.randint(first, (MICRO, N_CELLS, LOCAL_BLOCKS), 0, ROW_BLOCKS, dtype=jnp.int32)
    colblk = jax.random.randint(second, (MICRO, N_CELLS, LOCAL_BLOCKS), 0, ROW_BLOCKS, dtype=jnp.int32)
    return jnp.stack([rowblk, colblk], axis=-1)


def draw_halo_index(key, part):
    key = jax.random.fold_in(key, 14)
    first, second = jax.random.split(key)
    rowblk = jax.random.randint(first, (MICRO, N_CELLS, HALO_BLOCKS), 0, ROW_BLOCKS, dtype=jnp.int32)
    colblk = jax.random.randint(second, (MICRO, N_CELLS, HALO_BLOCKS), ROW_BLOCKS, ROW_BLOCKS + HALO_COLS, dtype=jnp.int32)
    return jnp.stack([rowblk, colblk], axis=-1)


def blocks_one_slab(key):
    first, second, third, fourth = jax.random.split(key, 4)
    own = jax.random.randint(first, (N_CELLS,), max(1, LOCAL_BLOCKS // 2), LOCAL_BLOCKS + 1, dtype=jnp.int32)
    far = jax.random.randint(second, (N_CELLS,), max(1, HALO_BLOCKS // 2), HALO_BLOCKS + 1, dtype=jnp.int32)
    own = own.at[jax.random.randint(third, (), 0, N_CELLS, dtype=jnp.int32)].set(LOCAL_BLOCKS)
    far = far.at[jax.random.randint(fourth, (), 0, N_CELLS, dtype=jnp.int32)].set(HALO_BLOCKS)
    return jnp.stack([own, far], axis=-1).astype(jnp.int32)


def draw_block_count(key, part):
    key = jax.random.fold_in(key, 15)
    return jax.vmap(blocks_one_slab)(jax.random.split(key, MICRO)).astype(jnp.int32)


def level_of(rng, extent, cuts, low, largest):
    factor_of = 1.0
    for dim, shards_of in cuts:
        heights = jax.random.uniform(jax.random.fold_in(jax.random.fold_in(rng, 6), dim), (shards_of,), jnp.float32, low / len(cuts), largest / len(cuts))
        factor_of = factor_of * jnp.repeat(jnp.exp(heights), extent[dim] // shards_of).reshape((-1,) + (1,) * (len(extent) - 1 - dim))
    return factor_of


def gaussian(stream_key, extent, width, most, cuts=(), held_as=jnp.bfloat16):
    values = jax.random.normal(stream_key, extent, jnp.float32) * width
    if len(cuts) > 0:
        values = level_of(stream_key, extent, cuts, -0.22, 0.18) * values
    return jnp.clip(values, min=-most, max=most).astype(held_as)


def setup_inputs(seed: int = 0) -> dict:
    seeds = jax.random.split(jax.random.key(seed), 12)
    feats = gaussian(seeds[0], (MICRO, TOTAL_ROWS, D), 1.0, 6.0, ((1, 128),))
    weights = gaussian(seeds[1], (LAYERS, D, D), D ** -0.5, 0.375, ((0, 4),))
    gains = jnp.clip(1.0 + 0.15 * jax.random.normal(seeds[2], (LAYERS, D), jnp.float32), 0.25, 1.75)
    send_rows = draw_send_rows(jax.random.fold_in(seeds[11], 71), 0)
    send_count = draw_send_count(jax.random.fold_in(seeds[11], 71), 0)
    local_index = draw_local_index(jax.random.fold_in(seeds[11], 71), 0)
    halo_index = draw_halo_index(jax.random.fold_in(seeds[11], 71), 0)
    block_count = draw_block_count(jax.random.fold_in(seeds[11], 71), 0)
    local_vals = gaussian(seeds[8], (MICRO, N_CELLS * LOCAL_BLOCKS, BLK, BLK), (BLK * 3) ** -0.5, 0.3125, ((1, 128),))
    halo_vals = gaussian(seeds[9], (MICRO, N_CELLS * HALO_BLOCKS, BLK, BLK), (BLK * 3) ** -0.5, 0.3125, ((1, 128),))
    cotangent = gaussian(seeds[10], (MICRO, TOTAL_ROWS, D), 1.0, 6.0, ((1, 128),))
    return dict(feats=feats, weights=weights, gains=gains, send_rows=send_rows, send_count=send_count, local_index=local_index, halo_index=halo_index, block_count=block_count, local_vals=local_vals, halo_vals=halo_vals, cotangent=cotangent)


EPS = 1e-05
COEF = 0.7978845608028654

def gelu_pair(inputs):
    inner = jnp.tanh(COEF * (inputs + 0.044715 * inputs * inputs * inputs))
    value = 0.5 * inputs * (1.0 + inner)
    slope = 0.5 * (1.0 + inner) + 0.5 * inputs * (1.0 - inner * inner) * COEF * (1.0 + 3.0 * 0.044715 * inputs * inputs)
    return (value, slope)

def block_product(source, index_list, values, live_count, offset, out_blocks):
    listed = index_list.shape[0]
    live_mask = (jnp.arange(listed) < live_count).astype(jnp.float32)
    masked = values.astype(jnp.float32) * live_mask[:, None, None]
    picked_tiles = source.reshape(-1, BLK, D)[index_list[:, 1] - offset].astype(jnp.float32)
    product = jnp.einsum('bij,bjd->bid', masked, picked_tiles, precision=lax.Precision.HIGHEST)
    select = (index_list[:, 0][None, :] == jnp.arange(out_blocks)[:, None]).astype(jnp.float32)
    summed = jnp.einsum('rb,bid->rid', select, product, precision=lax.Precision.HIGHEST)
    return summed.reshape(out_blocks * BLK, D)

def block_transpose(grad_rows, index_list, values, live_count, offset, out_blocks):
    listed = index_list.shape[0]
    live_mask = (jnp.arange(listed) < live_count).astype(jnp.float32)
    masked = values.astype(jnp.float32) * live_mask[:, None, None]
    picked_tiles = grad_rows.reshape(-1, BLK, D)[index_list[:, 0]].astype(jnp.float32)
    product = jnp.einsum('bij,bid->bjd', masked, picked_tiles, precision=lax.Precision.HIGHEST)
    select = ((index_list[:, 1] - offset)[None, :] == jnp.arange(out_blocks)[:, None]).astype(jnp.float32)
    summed = jnp.einsum('cb,bjd->cjd', select, product, precision=lax.Precision.HIGHEST)
    return summed.reshape(out_blocks * BLK, D)

def activate(summed, gain_row):
    inverse = lax.rsqrt(lax.optimization_barrier(jnp.mean(summed * summed, axis=-1, keepdims=True)) + EPS)
    normed = summed * inverse * gain_row
    value, slope = gelu_pair(normed)
    return (inverse, value.astype(jnp.bfloat16), slope)

def run_slab(feats, weights, gains, send_rows, send_count, local_index, halo_index, block_count, local_vals, halo_vals, cotangent):
    live_slot = jnp.arange(PEER_SLOTS)[None, None, :] < send_count[:, :, None]
    local_tiles = local_vals.reshape(N_CELLS, LOCAL_BLOCKS, BLK, BLK)
    halo_tiles = halo_vals.reshape(N_CELLS, HALO_BLOCKS, BLK, BLK)

    def halo_of(current):
        picked = jax.vmap(lambda rows_here, index_here: rows_here[index_here])(current, send_rows)
        picked = jnp.where(live_slot[..., None], picked, jnp.zeros_like(picked))
        return picked.transpose(1, 0, 2, 3).reshape(N_CELLS, HALO_ROWS, D)

    def aggregate(current):
        received = halo_of(current)

        def one_owner(items):
            source, incoming, local_list, halo_list, counts, own_tiles, far_tiles = items
            extended = jnp.concatenate([source, incoming], axis=0)
            return block_product(extended, local_list, own_tiles, counts[0], 0, ROW_BLOCKS) + block_product(extended, halo_list, far_tiles, counts[1], 0, ROW_BLOCKS)
        return lax.map(one_owner, (current, received, local_index, halo_index, block_count, local_tiles, halo_tiles))
    current = feats.reshape(N_CELLS, ROWS_DEV, D)
    saved_sums = []
    outputs = []
    for layer in range(LAYERS):
        summed = aggregate(current)
        inverse, activated, slope = activate(summed, gains[layer])
        branch = jnp.dot(activated.reshape(-1, D), weights[layer], preferred_element_type=jnp.float32)
        result = (current.astype(jnp.float32) + branch.reshape(N_CELLS, ROWS_DEV, D)).astype(jnp.bfloat16)
        saved_sums.append(summed)
        outputs.append(result.reshape(TOTAL_ROWS, D))
        current = result
    upstream = cotangent.reshape(N_CELLS, ROWS_DEV, D)
    grads_in = [None] * LAYERS
    grads_weight = [None] * LAYERS
    grads_gain = [None] * LAYERS
    for layer in reversed(range(LAYERS)):
        summed = saved_sums[layer]
        gain_row = gains[layer]
        inverse, activated, slope = activate(summed, gain_row)
        flat_up = upstream.reshape(-1, D)
        grads_weight[layer] = jnp.dot(activated.reshape(-1, D).T, flat_up, preferred_element_type=jnp.float32)
        grad_act = jnp.dot(flat_up, weights[layer].T, preferred_element_type=jnp.float32).reshape(N_CELLS, ROWS_DEV, D)
        grad_normed = grad_act * slope
        grads_gain[layer] = lax.optimization_barrier(jnp.sum(grad_normed * summed * inverse, axis=(0, 1)))
        grad_scaled = grad_normed * gain_row
        grad_summed = (inverse * (grad_scaled - summed * inverse * inverse * lax.optimization_barrier(jnp.mean(grad_scaled * summed, axis=-1, keepdims=True)))).astype(jnp.bfloat16)

        def one_back(items):
            grad_rows, local_list, halo_list, counts, own_tiles, far_tiles = items
            own_part = block_transpose(grad_rows, local_list, own_tiles, counts[0], 0, ROW_BLOCKS)
            far_part = block_transpose(grad_rows, halo_list, far_tiles, counts[1], ROW_BLOCKS, HALO_COLS).astype(jnp.bfloat16)
            return (own_part, far_part)
        own_parts, far_parts = lax.map(one_back, (grad_summed, local_index, halo_index, block_count, local_tiles, halo_tiles))
        returned = far_parts.reshape(N_CELLS, N_CELLS, PEER_SLOTS, D).transpose(1, 0, 2, 3)
        returned = jnp.where(live_slot[..., None], returned, jnp.zeros_like(returned)).astype(jnp.float32)
        spread = jax.vmap(lambda index_here, rows_here: jnp.zeros((ROWS_DEV, D), jnp.float32).at[index_here.reshape(-1)].add(rows_here.reshape(-1, D)))(send_rows, returned)
        result = (upstream.astype(jnp.float32) + own_parts + spread).astype(jnp.bfloat16)
        grads_in[layer] = result.reshape(TOTAL_ROWS, D)
        upstream = result
    return (outputs, grads_in, grads_weight, grads_gain)

def reference(feats, weights, gains, send_rows, send_count, local_index, halo_index, block_count, local_vals, halo_vals, cotangent):
    scale = 1.0 / math.sqrt(MICRO * TOTAL_ROWS)
    outs_all = []
    grads_all = []
    weight_total = [jnp.zeros((D, D), jnp.float32) for layer in range(LAYERS)]
    gain_total = [jnp.zeros((D,), jnp.float32) for layer in range(LAYERS)]
    for slab in range(MICRO):
        outputs, grads_in, grads_weight, grads_gain = run_slab(feats[slab], weights, gains, send_rows[slab], send_count[slab], local_index[slab], halo_index[slab], block_count[slab], local_vals[slab], halo_vals[slab], cotangent[slab])
        outs_all.append(jnp.stack(outputs))
        grads_all.append(jnp.stack(grads_in))
        weight_total = [weight_total[layer] + grads_weight[layer] for layer in range(LAYERS)]
        gain_total = [gain_total[layer] + grads_gain[layer] for layer in range(LAYERS)]
    layer_outputs = jnp.stack(outs_all, axis=1)
    input_grads = jnp.stack(grads_all, axis=1)
    return (layer_outputs, input_grads, jnp.stack(weight_total) * scale, jnp.stack(gain_total) * scale)
```

```python
import functools
import math

import jax
import jax.numpy as jnp
from jax import lax
from jax.experimental import pallas as pl
from jax.experimental.pallas import tpu as pltpu
from jax.sharding import PartitionSpec as P

EPS = 1e-05
COEF = 0.7978845608028654
CUBIC = 0.044715
LAYERS = 4
D = 256
ROWS = 256
OWNERS = 128
BLK = 128
BF = jnp.bfloat16
F32 = jnp.float32
MESH = pl.DeviceIdType.MESH
SCALE = 1.0 / math.sqrt(OWNERS * ROWS)


def mm(a, b):
    return jnp.dot(a, b, preferred_element_type=F32)


def mm_nt(a, b):
    return lax.dot_general(a, b, (((1,), (1,)), ((), ())), preferred_element_type=F32)


def mm_tn(a, b):
    return lax.dot_general(a, b, (((0,), (0,)), ((), ())), preferred_element_type=F32)


def turned(tile):
    rows = []
    for i in range(2):
        rows.append(
            jnp.concatenate(
                [tile[j * BLK : (j + 1) * BLK, i * BLK : (i + 1) * BLK].T for j in range(2)], axis=1
            )
        )
    return jnp.concatenate(rows, axis=0)


def kernel(
    feats,
    weight,
    near,
    far,
    cot,
    meta,
    out_x,
    out_g,
    out_w,
    out_gg,
    xs,
    gs,
    ws,
    near_here,
    far_here,
    meta_here,
    meta_all,
    pick,
    pick_t,
    adj,
    adj_t,
    halo,
    halo_t,
    sent,
    got,
    normed,
    slopes,
    inverse,
    acts,
    upgrad,
    wg_out,
    wg_in,
    zb_out,
    zb_in,
    wc_out,
    gg_out,
    gg_in,
    ggz_out,
    ggz_in,
    filler,
    sem_rel_send,
    sem_rel,
    sem_w_send,
    sem_w,
    sem_m_send,
    sem_m,
    sem_send,
    sem_got,
    sem_a_send,
    sem_a,
    sem_b_send,
    sem_b,
    sem_c_send,
    sem_c,
    sem_gg_send,
    sem_gg,
    sem_ggz_send,
    sem_ggz,
    sem_o_send,
    sem_o,
):
    x = lax.axis_index("segment")
    q = lax.axis_index("cells")
    z = q // 8
    wv = q % 8
    y = wv // 2
    core = wv % 2
    blk = z // 4
    zl = z % 4
    me = (4 * x + zl) * 8 + wv
    diag = x == blk
    not_diag = x != blk

    def dev(xx, zz, ww):
        return (xx, (4 * blk + zz) * 8 + ww)

    def remote(src, dst, send, recv, device):
        return pltpu.make_async_remote_copy(
            src, dst, send, recv, device_id=device, device_id_type=MESH
        )

    def wait_for(ref, sem):
        pltpu.make_async_copy(ref, ref, sem).wait()

    barrier = pltpu.get_barrier_semaphore()

    @pl.when(not_diag)
    def _():
        for xx in range(4):
            pl.semaphore_signal(
                barrier, inc=1, device_id=(xx, (4 * x + zl) * 8 + wv), device_id_type=MESH
            )

    def greet(i, carry):
        k = 127 - i
        xx = (x + k // 32) % 4
        zz = (zl + (k // 8) % 4) % 4
        ww = (wv + k % 8) % 8
        pl.semaphore_signal(barrier, inc=1, device_id=dev(xx, zz, ww), device_id_type=MESH)
        return carry

    lax.fori_loop(0, 127, greet, 0)
    pl.semaphore_wait(barrier, 130)

    def relocate(src, dst, rows, k):
        part = src.at[pl.ds(rows * x, rows)]
        there = dst.at[pl.ds(rows * x, rows)]
        for bb in range(4):

            @pl.when(jnp.logical_and(diag, blk == bb))
            def _():
                pltpu.make_async_copy(part, there, sem_rel.at[k]).start()

            @pl.when(jnp.logical_not(jnp.logical_and(diag, blk == bb)))
            def _():
                remote(
                    part,
                    there,
                    sem_rel_send.at[k],
                    sem_rel.at[k],
                    (blk, (4 * bb + zl) * 8 + wv),
                ).start()

    def relocated(src, rows, k):
        @pl.when(diag)
        def _():
            wait_for(src.at[pl.ds(0, 3 * rows)], sem_rel_send.at[k])

        @pl.when(not_diag)
        def _():
            wait_for(src.at[pl.ds(0, 4 * rows)], sem_rel_send.at[k])

    @pl.when(diag)
    def _():
        for bb in range(4):

            @pl.when(blk == bb)
            def _():
                pltpu.make_async_copy(meta, meta_here, sem_rel.at[4]).start()

            @pl.when(blk != bb)
            def _():
                remote(
                    meta,
                    meta_here,
                    sem_rel_send.at[4],
                    sem_rel.at[4],
                    (blk, (4 * bb + zl) * 8 + wv),
                ).start()

    relocate(feats, xs.at[0], 64, 0)
    relocate(near, near_here, 128, 1)
    relocate(far, far_here, 64, 2)
    for dx in (2, 1, 3):
        remote(meta, meta_all.at[x], sem_m_send, sem_m, ((x + dx) % 4, q)).start()
    pltpu.make_async_copy(meta, meta_all.at[x], sem_m).start()

    def share_weights():
        for l in range(LAYERS):

            @pl.when(x == l)
            def _():
                for dx in (2, 1, 3):
                    remote(
                        weight, ws.at[l], sem_w_send, sem_w.at[l], ((x + dx) % 4, q)
                    ).start()
                pltpu.make_async_copy(weight, ws.at[l], sem_w.at[l]).start()

    def send_all(r, matrix, source):
        for dx in (2, 1, 3, 0):
            xx = (x + dx) % 4
            rows = mm(matrix[pl.ds(pl.multiple_of(64 * xx, 64), 64), :], source)
            sent[r, pl.ds(32 * xx, 32)] = rows.astype(BF).reshape(32, 2, D)

            def to_z(i, carry):
                zz = lax.rem(zl + 3 - i, 4)
                for dy in (2, 1, 3, 0):
                    for dc in (1, 0):
                        ww = ((y + dy) % 4) * 2 + (core + dc) % 2
                        v = (4 * xx + zz) * 8 + ww
                        if dx == 0 and dy == 0 and dc == 0:

                            @pl.when(v != me)
                            def _():
                                remote(
                                    sent.at[r, v],
                                    got.at[r, me],
                                    sem_send.at[r],
                                    sem_got.at[r],
                                    dev(xx, zz, ww),
                                ).start()

                            @pl.when(v == me)
                            def _():
                                pltpu.make_async_copy(
                                    sent.at[r, v], got.at[r, v], sem_got.at[r]
                                ).start()
                        else:
                            remote(
                                sent.at[r, v],
                                got.at[r, me],
                                sem_send.at[r],
                                sem_got.at[r],
                                dev(xx, zz, ww),
                            ).start()
                return carry

            lax.fori_loop(0, 4, to_z, 0)

    def receive(r):
        wait_for(got.at[r], sem_got.at[r])
        return got[r].reshape(OWNERS * 2, D)

    def emit(value, out, kind, l):
        @pl.when(jnp.logical_and(diag, x == l))
        def _():
            pltpu.make_async_copy(value, out, sem_o.at[kind]).start()

        @pl.when(jnp.logical_and(diag, x != l))
        def _():
            remote(value, out, sem_o_send.at[kind, l], sem_o.at[kind], (l, q)).start()

    wait_for(meta_here, sem_rel.at[4])
    targets = meta_here[0:1, :]
    rows_iota = lax.broadcasted_iota(jnp.int32, (ROWS, 2 * OWNERS), 0).astype(F32)
    hot = jnp.where(rows_iota == targets, 1.0, 0.0)
    pick_t[...] = hot.astype(BF)
    pick[...] = turned(hot).astype(BF)
    wait_for(xs.at[0], sem_rel.at[0])

    def build_adjacency():
        wait_for(near_here, sem_rel.at[1])
        wait_for(far_here, sem_rel.at[2])

        def entry(k):
            return meta_here[1:2, k : k + 1]

        for listed, base, live_at, shift, values, target, target_t in (
            (4, 0, 12, 0, near_here, adj, adj_t),
            (2, 8, 13, 2, far_here, halo, halo_t),
        ):
            tiles = [values[i * BLK : (i + 1) * BLK, :].astype(F32) for i in range(listed)]
            for rb in range(2):
                for cb in range(2):
                    total = jnp.zeros((BLK, BLK), F32)
                    for i in range(listed):
                        hit = jnp.where(
                            jnp.logical_and(
                                jnp.logical_and(
                                    entry(base + 2 * i) == float(rb),
                                    entry(base + 2 * i + 1) == float(cb + shift),
                                ),
                                entry(live_at) > float(i),
                            ),
                            1.0,
                            0.0,
                        )
                        total = total + tiles[i] * hit
                    target[rb * BLK : (rb + 1) * BLK, cb * BLK : (cb + 1) * BLK] = total.astype(BF)
                    target_t[cb * BLK : (cb + 1) * BLK, rb * BLK : (rb + 1) * BLK] = (
                        total.T.astype(BF)
                    )

    def gain_of(l):
        return meta_all[l, 2:3, :]

    def norm_of(total):
        inv = lax.rsqrt(jnp.mean(total * total, axis=-1, keepdims=True) + EPS)
        return inv, total * inv

    def inner_of(v):
        return jnp.tanh(COEF * (v + CUBIC * v * v * v))

    def slope_of(v, inner):
        return 0.5 * (1.0 + inner) + 0.5 * v * (1.0 - inner * inner) * COEF * (
            1.0 + 3.0 * CUBIC * v * v
        )

    for l in range(LAYERS):
        send_all(l, pick, xs[l])
        if l == 0:
            relocate(cot, gs.at[LAYERS], 64, 3)
            share_weights()
            build_adjacency()
            wait_for(meta_all, sem_m)
        if l > 0:
            emit(xs.at[l], out_x, 0, l - 1)
            v = normed[l - 1] * gain_of(l - 1)
            slopes[l - 1] = slope_of(v, inner_of(v))
        wait_for(ws.at[l], sem_w.at[l])
        if l == LAYERS - 1:
            wait_for(gs.at[LAYERS], sem_rel.at[3])
            upgrad[...] = mm_nt(gs[LAYERS], ws[l])
        own = mm(adj[...], xs[l])
        total = own + mm(halo[...], receive(l))
        inv, nh = norm_of(total)
        v = nh * gain_of(l)
        inner = inner_of(v)
        inverse[l] = jnp.broadcast_to(inv, (ROWS, BLK))
        normed[l] = nh
        acts[l] = (0.5 * v * (1.0 + inner)).astype(BF)
        if l < LAYERS - 1:
            xs[l + 1] = (xs[l].astype(F32) + mm(acts[l], ws[l])).astype(BF)
        else:
            slopes[l] = slope_of(v, inner)

    def tiles_out(l):
        partial = mm_tn(acts[l], gs[l + 1]).astype(BF)
        for i in range(32):
            rt, ct = i // 2, i % 2
            wg_out[l, i] = partial[16 * rt : 16 * rt + 16, BLK * ct : BLK * ct + BLK]
        here = x * 8 + wv

        def to_x(i, carry):
            xx = (x + 3 - i) % 4
            for dw in range(8):
                ww = (wv + dw) % 8
                there = xx * 8 + ww
                if dw == 0:

                    @pl.when(there == here)
                    def _():
                        pltpu.make_async_copy(
                            wg_out.at[l, there], wg_in.at[l, here], sem_a.at[l]
                        ).start()

                    @pl.when(there != here)
                    def _():
                        remote(
                            wg_out.at[l, there],
                            wg_in.at[l, here],
                            sem_a_send.at[l],
                            sem_a.at[l],
                            dev(xx, zl, ww),
                        ).start()
                else:
                    remote(
                        wg_out.at[l, there],
                        wg_in.at[l, here],
                        sem_a_send.at[l],
                        sem_a.at[l],
                        dev(xx, zl, ww),
                    ).start()
            return carry

        lax.fori_loop(0, 4, to_x, 0)

    def tiles_z(l):
        wait_for(wg_in.at[l], sem_a.at[l])
        total = wg_in[l, 0].astype(F32)
        for i in range(1, 32):
            total = total + wg_in[l, i].astype(F32)
        zb_out[l] = total
        for dz in (3, 2, 1):
            remote(
                zb_out.at[l],
                zb_in.at[l, zl],
                sem_b_send.at[l],
                sem_b.at[l],
                dev(x, (zl + dz) % 4, wv),
            ).start()
        pltpu.make_async_copy(zb_out.at[l], zb_in.at[l, zl], sem_b.at[l]).start()

    def tiles_home(l):
        wait_for(zb_in.at[l], sem_b.at[l])
        wc_out[l] = (zb_in[l, 0] + zb_in[l, 1] + zb_in[l, 2] + zb_in[l, 3]) * SCALE
        place = out_w.at[
            pl.ds(pl.multiple_of(16 * (4 * x + wv // 2), 16), 16),
            pl.ds(pl.multiple_of(BLK * (wv % 2), BLK), BLK),
        ]
        for dw in (4, 5, 3, 2, 6, 7, 1, 0):
            ww = (wv + dw) % 8
            if dw == 0:

                @pl.when(x == l)
                def _():
                    pltpu.make_async_copy(wc_out.at[l], place, sem_c).start()

                @pl.when(x != l)
                def _():
                    remote(wc_out.at[l], place, sem_c_send.at[l], sem_c, dev(l, zl, ww)).start()
            else:
                remote(wc_out.at[l], place, sem_c_send.at[l], sem_c, dev(l, zl, ww)).start()

    def gains_out(l):
        for dw in (4, 5, 3, 2, 6, 7, 1, 0):
            ww = (wv + dw) % 8
            place = gg_in.at[x * 8 + wv]
            if dw == 0:

                @pl.when(x == l)
                def _():
                    pltpu.make_async_copy(gg_out.at[l], place, sem_gg).start()

                @pl.when(x != l)
                def _():
                    remote(gg_out.at[l], place, sem_gg_send.at[l], sem_gg, dev(l, zl, ww)).start()
            else:
                remote(gg_out.at[l], place, sem_gg_send.at[l], sem_gg, dev(l, zl, ww)).start()

    for l in reversed(range(LAYERS)):
        r = 2 * LAYERS - 1 - l
        if l < LAYERS - 1:
            if l == 0:
                tiles_out(l)
            upgrad[...] = mm_nt(gs[l + 1], ws[l])
        nh = normed[l]
        m = upgrad[...] * slopes[l]
        s = m * gain_of(l)
        t = jnp.mean(s * nh, axis=-1, keepdims=True)
        down = (inverse[l][:, 0:1] * (s - nh * t)).astype(BF)
        send_all(r, halo_t, down)
        gg_out[l] = jnp.sum(m * nh, axis=0, keepdims=True)
        gains_out(l)
        if l == LAYERS - 1:
            xs[LAYERS] = (xs[l].astype(F32) + mm(acts[l], ws[l])).astype(BF)
            emit(xs.at[LAYERS], out_x, 0, l)
        else:
            emit(gs.at[l + 1], out_g, 1, l + 1)
        if l > 0:
            tiles_out(l)
        own = mm(adj_t[...], down)
        if l + 1 < LAYERS:
            tiles_z(l + 1)
        if l + 2 < LAYERS:
            tiles_home(l + 2)
        if l == 0:
            tiles_home(1)
            tiles_z(0)
        gs[l] = (gs[l + 1].astype(F32) + own + mm(pick_t[...], receive(r))).astype(BF)

    emit(gs.at[0], out_g, 1, 0)
    wait_for(gg_in, sem_gg)
    ggz_out[...] = jnp.sum(gg_in[...], axis=0)
    for dz in (3, 2, 1):
        remote(
            ggz_out, ggz_in.at[zl], sem_ggz_send, sem_ggz, dev(x, (zl + dz) % 4, wv)
        ).start()
    pltpu.make_async_copy(ggz_out, ggz_in.at[zl], sem_ggz).start()
    tiles_home(0)
    wait_for(ggz_in, sem_ggz)
    out_gg[...] = jnp.sum(ggz_in[...], axis=0) * SCALE

    wait_for(out_x, sem_o.at[0])
    wait_for(out_g, sem_o.at[1])
    wait_for(out_w, sem_c)
    relocated(feats, 64, 0)
    relocated(near, 128, 1)
    relocated(far, 64, 2)
    relocated(cot, 64, 3)

    @pl.when(diag)
    def _():
        wait_for(meta_all.at[pl.ds(0, 3)], sem_rel_send.at[4])

    wait_for(meta_all.at[pl.ds(0, 3)], sem_m_send)
    wait_for(ws.at[pl.ds(0, 3)], sem_w_send)
    for r in range(2 * LAYERS):
        wait_for(sent.at[r, pl.ds(0, OWNERS - 1)], sem_send.at[r])
    for l in range(LAYERS):
        wait_for(wg_in.at[l, pl.ds(0, 31)], sem_a_send.at[l])
        wait_for(zb_in.at[l, pl.ds(0, 3)], sem_b_send.at[l])

        @pl.when(x == l)
        def _():
            wait_for(filler.at[pl.ds(0, 7)], sem_c_send.at[l])
            wait_for(gg_in.at[pl.ds(0, 7)], sem_gg_send.at[l])

        @pl.when(x != l)
        def _():
            wait_for(filler, sem_c_send.at[l])
            wait_for(gg_in.at[pl.ds(0, 8)], sem_gg_send.at[l])

        @pl.when(jnp.logical_and(diag, x != l))
        def _():
            wait_for(gs.at[l], sem_o_send.at[0, l])
            wait_for(gs.at[l], sem_o_send.at[1, l])

    wait_for(ggz_in.at[pl.ds(0, 3)], sem_ggz_send)


def on_device(
    feats,
    weights,
    gains,
    send_rows,
    send_count,
    local_index,
    halo_index,
    block_count,
    local_vals,
    halo_vals,
    cotangent,
):
    live = jnp.arange(2)[None, :] < send_count[0, 0][:, None]
    targets = jnp.where(live, send_rows[0, 0], -1).astype(F32).reshape(1, 2 * OWNERS)
    lists = jnp.concatenate(
        [local_index.reshape(-1), halo_index.reshape(-1), block_count.reshape(-1)]
    ).astype(F32)
    lists = jnp.pad(lists, (0, D - lists.shape[0]))[None]
    meta = jnp.concatenate([targets, lists, gains, jnp.zeros((5, D), F32)], axis=0)
    any_spec = pl.BlockSpec(memory_space=pl.ANY)
    vmem_spec = pl.BlockSpec(memory_space=pltpu.VMEM)
    dma = pltpu.SemaphoreType.DMA
    out_x, out_g, out_w, out_gg = pl.pallas_call(
        kernel,
        out_shape=(
            jax.ShapeDtypeStruct((ROWS, D), BF),
            jax.ShapeDtypeStruct((ROWS, D), BF),
            jax.ShapeDtypeStruct((D, D), F32),
            jax.ShapeDtypeStruct((1, D), F32),
        ),
        in_specs=[any_spec] * 6,
        out_specs=(any_spec, any_spec, any_spec, vmem_spec),
        scratch_shapes=[
            pltpu.VMEM((LAYERS + 1, ROWS, D), BF),
            pltpu.VMEM((LAYERS + 1, ROWS, D), BF),
            pltpu.VMEM((LAYERS, D, D), BF),
            pltpu.VMEM((4 * BLK, BLK), BF),
            pltpu.VMEM((2 * BLK, BLK), BF),
            pltpu.VMEM((8, D), F32),
            pltpu.VMEM((LAYERS, 8, D), F32),
            pltpu.VMEM((2 * OWNERS, ROWS), BF),
            pltpu.VMEM((ROWS, 2 * OWNERS), BF),
            pltpu.VMEM((ROWS, ROWS), BF),
            pltpu.VMEM((ROWS, ROWS), BF),
            pltpu.VMEM((ROWS, 2 * OWNERS), BF),
            pltpu.VMEM((2 * OWNERS, ROWS), BF),
            pltpu.VMEM((2 * LAYERS, OWNERS, 2, D), BF),
            pltpu.VMEM((2 * LAYERS, OWNERS, 2, D), BF),
            pltpu.VMEM((LAYERS, ROWS, D), F32),
            pltpu.VMEM((LAYERS, ROWS, D), F32),
            pltpu.VMEM((LAYERS, ROWS, BLK), F32),
            pltpu.VMEM((LAYERS, ROWS, D), BF),
            pltpu.VMEM((ROWS, D), F32),
            pltpu.VMEM((LAYERS, 32, 16, BLK), BF),
            pltpu.VMEM((LAYERS, 32, 16, BLK), BF),
            pltpu.VMEM((LAYERS, 16, BLK), F32),
            pltpu.VMEM((LAYERS, 4, 16, BLK), F32),
            pltpu.VMEM((LAYERS, 16, BLK), F32),
            pltpu.VMEM((LAYERS, 1, D), F32),
            pltpu.VMEM((32, 1, D), F32),
            pltpu.VMEM((1, D), F32),
            pltpu.VMEM((4, 1, D), F32),
            pltpu.VMEM((8, 16, BLK), F32),
            dma((5,)),
            dma((5,)),
            dma,
            dma((LAYERS,)),
            dma,
            dma,
            dma((2 * LAYERS,)),
            dma((2 * LAYERS,)),
            dma((LAYERS,)),
            dma((LAYERS,)),
            dma((LAYERS,)),
            dma((LAYERS,)),
            dma((LAYERS,)),
            dma,
            dma((LAYERS,)),
            dma,
            dma,
            dma,
            dma((2, LAYERS)),
            dma((2,)),
        ],
        compiler_params=pltpu.CompilerParams(
            collective_id=0, has_side_effects=True, vmem_limit_bytes=48 * 1024 * 1024
        ),
    )(
        feats[0],
        weights[0],
        local_vals.reshape(4 * BLK, BLK),
        halo_vals.reshape(2 * BLK, BLK),
        cotangent[0],
        meta,
    )
    return out_x[None, None], out_g[None, None], out_w[None], out_gg


def solution(mesh):
    in_specs = (
        P(None, "cells", None),
        P("segment", None, None),
        P("segment", None),
        P(None, "cells", None, None),
        P(None, "cells", None),
        P(None, "cells", None, None),
        P(None, "cells", None, None),
        P(None, "cells", None),
        P(None, "cells", None, None),
        P(None, "cells", None, None),
        P(None, "cells", None),
    )
    out_specs = (
        P("segment", None, "cells", None),
        P("segment", None, "cells", None),
        P("segment", None, None),
        P("segment", None),
    )
    return jax.shard_map(
        on_device, mesh=mesh, in_specs=in_specs, out_specs=out_specs, check_vma=False
    )
```

```python
import functools
import math

import jax
import jax.numpy as jnp
from jax import lax
from jax.experimental import pallas as pl
from jax.experimental.pallas import tpu as pltpu
from jax.sharding import PartitionSpec as P

EPS = 1e-05
COEF = 0.7978845608028654
CUBIC = 0.044715
LAYERS = 4
D = 256
ROWS = 256
OWNERS = 128
BLK = 128
BF = jnp.bfloat16
F32 = jnp.float32
MESH = pl.DeviceIdType.MESH
SCALE = 1.0 / math.sqrt(OWNERS * ROWS)


def mm(a, b):
    return jnp.dot(a, b, preferred_element_type=F32)


def mm_nt(a, b):
    return lax.dot_general(a, b, (((1,), (1,)), ((), ())), preferred_element_type=F32)


def mm_tn(a, b):
    return lax.dot_general(a, b, (((0,), (0,)), ((), ())), preferred_element_type=F32)


def turned(tile):
    rows = []
    for i in range(2):
        rows.append(
            jnp.concatenate(
                [tile[j * BLK : (j + 1) * BLK, i * BLK : (i + 1) * BLK].T for j in range(2)], axis=1
            )
        )
    return jnp.concatenate(rows, axis=0)


def kernel(
    feats,
    weight,
    near,
    far,
    cot,
    rows_in,
    count_in,
    near_in,
    far_in,
    live_in,
    gains_in,
    out_x,
    out_g,
    out_w,
    out_gg,
    xs,
    gs,
    ws,
    near_here,
    far_here,
    rows_v,
    count_v,
    near_v,
    far_v,
    live_v,
    gains_v,
    meta,
    meta_here,
    meta_all,
    pick,
    pick_t,
    pick_home_t,
    adj,
    adj_t,
    halo,
    halo_t,
    sent,
    got,
    normed,
    slopes,
    inverse,
    acts,
    upgrad,
    wg_out,
    wg_in,
    zb_out,
    zb_in,
    wc_out,
    gg_out,
    gg_in,
    base_out,
    base_in,
    filler,
    sem_in,
    sem_rel_send,
    sem_rel,
    sem_w_send,
    sem_w,
    sem_m_send,
    sem_m,
    sem_send,
    sem_got,
    sem_a_send,
    sem_a,
    sem_b_send,
    sem_b,
    sem_c_send,
    sem_c,
    sem_gg_send,
    sem_gg,
    sem_base_send,
    sem_base,
    sem_o_send,
    sem_o,
):
    x = lax.axis_index("segment")
    q = lax.axis_index("cells")
    z = q // 8
    wv = q % 8
    y = wv // 2
    core = wv % 2
    blk = z // 4
    zl = z % 4

    def seat(xx, zz):
        aside = jnp.where(lax.rem(blk + 4 - xx, 4) == 2, 1, 0)
        return zz + aside * (1 - 2 * lax.rem(zz, 2))

    zo = seat(x, zl)
    me = (4 * x + zo) * 8 + wv
    diag = x == blk
    not_diag = x != blk

    def dev(xx, zz, ww):
        return (xx, (4 * blk + zz) * 8 + ww)

    def remote(src, dst, send, recv, device):
        return pltpu.make_async_remote_copy(
            src, dst, send, recv, device_id=device, device_id_type=MESH
        )

    def wait_for(ref, sem):
        pltpu.make_async_copy(ref, ref, sem).wait()

    small = [
        pltpu.make_async_copy(there, here, sem_in.at[i])
        for i, (there, here) in enumerate(
            (
                (rows_in, rows_v),
                (count_in, count_v),
                (near_in, near_v),
                (far_in, far_v),
                (live_in, live_v),
                (gains_in, gains_v),
            )
        )
    ]
    for copy in small:
        copy.start()

    seg_of = [lax.rem(x + i, 4) for i in range(4)]
    upper = zl // 2
    z_near = zl + 1 - 2 * lax.rem(zl, 2)
    z_by_distance = (3 - 3 * upper, 2 - upper, z_near, zl)
    base_of = [(4 * blk + zz) * 8 for zz in z_by_distance]
    lane_of = {
        (dy, dc): lax.rem(y + dy, 4) * 2 + (lax.rem(core + 1, 2) if dc else core)
        for dy in range(4)
        for dc in range(2)
    }
    in_order = sorted(
        ((i, dy, dc) for i in range(4) for dy in range(4) for dc in range(2)),
        key=lambda t: -((2.5, 1.5, 1.0, 0.0)[t[0]] + (0, 1, 2, 1)[t[1]] + 0.1 * t[2]),
    )

    barrier = pltpu.get_barrier_semaphore()

    @pl.when(not_diag)
    def _():
        for xx in range(4):
            pl.semaphore_signal(
                barrier, inc=1, device_id=(xx, (4 * x + zo) * 8 + wv), device_id_type=MESH
            )

    for dx in (2, 1, 3, 0):
        for i, dy, dc in in_order:
            if (dx, i, dy, dc) != (0, 3, 0, 0):
                pl.semaphore_signal(
                    barrier,
                    inc=1,
                    device_id=(seg_of[dx], base_of[i] + lane_of[dy, dc]),
                    device_id_type=MESH,
                )

    for copy in small:
        copy.wait()
    meta[...] = jnp.zeros_like(meta)
    for k in range(2):
        wanted = jnp.where(count_v[...] > k, rows_v[k : k + 1, :], -1)
        meta[0:1, k * OWNERS : (k + 1) * OWNERS] = wanted.astype(F32)
    meta[2:4, 0:4] = near_v[...].astype(F32)
    meta[4:6, 0:2] = far_v[...].astype(F32)
    meta[6:7, 0:2] = live_v[...].astype(F32)
    meta[7:8, :] = gains_v[...]
    pl.semaphore_wait(barrier, 130)

    def relocate(src, dst, rows, k):
        part = src.at[pl.ds(rows * x, rows)]
        there = dst.at[pl.ds(rows * x, rows)]
        for bb in range(4):
            there_z = jnp.where(lax.rem(bb + 4 - blk, 4) == 2, z_near, zl)

            @pl.when(jnp.logical_and(diag, blk == bb))
            def _():
                pltpu.make_async_copy(part, there, sem_rel.at[k]).start()

            @pl.when(jnp.logical_not(jnp.logical_and(diag, blk == bb)))
            def _():
                remote(
                    part,
                    there,
                    sem_rel_send.at[k],
                    sem_rel.at[k],
                    (blk, (4 * bb + there_z) * 8 + wv),
                ).start()

    def relocated(src, rows, k):
        @pl.when(diag)
        def _():
            wait_for(src.at[pl.ds(0, 3 * rows)], sem_rel_send.at[k])

        @pl.when(not_diag)
        def _():
            wait_for(src.at[pl.ds(0, 4 * rows)], sem_rel_send.at[k])

    @pl.when(diag)
    def _():
        for bb in range(4):
            there_z = jnp.where(lax.rem(bb + 4 - blk, 4) == 2, z_near, zl)

            @pl.when(blk == bb)
            def _():
                pltpu.make_async_copy(meta, meta_here, sem_rel.at[4]).start()

            @pl.when(blk != bb)
            def _():
                remote(
                    meta,
                    meta_here,
                    sem_rel_send.at[4],
                    sem_rel.at[4],
                    (blk, (4 * bb + there_z) * 8 + wv),
                ).start()

    relocate(feats, xs.at[0], 64, 0)
    relocate(near, near_here, 128, 1)
    relocate(far, far_here, 64, 2)
    for dx in (2, 1, 3):
        remote(meta, meta_all.at[x], sem_m_send, sem_m, ((x + dx) % 4, q)).start()
    pltpu.make_async_copy(meta, meta_all.at[x], sem_m).start()

    def share_weights():
        for l in range(LAYERS):

            @pl.when(x == l)
            def _():
                for dx in (2, 1, 3):
                    remote(
                        weight, ws.at[l], sem_w_send, sem_w.at[l], ((x + dx) % 4, q)
                    ).start()
                pltpu.make_async_copy(weight, ws.at[l], sem_w.at[l]).start()

    def send_all(r, matrix, source):
        for dx in (2, 1, 3, 0):
            xx = seg_of[dx]
            rows = mm(matrix[pl.ds(pl.multiple_of(64 * xx, 64), 64), :], source)
            sent[r, pl.ds(32 * xx, 32)] = rows.astype(BF).reshape(32, 2, D)

            for i, dy, dc in in_order:
                cell = base_of[i] + lane_of[dy, dc]
                v = 32 * xx + 8 * seat(xx, z_by_distance[i]) + lane_of[dy, dc]
                if (dx, i, dy, dc) == (0, 3, 0, 0):
                    pltpu.make_async_copy(sent.at[r, v], got.at[r, v], sem_got.at[r]).start()
                else:
                    remote(
                        sent.at[r, v], got.at[r, me], sem_send.at[r], sem_got.at[r], (xx, cell)
                    ).start()

    def receive(r):
        wait_for(got.at[r], sem_got.at[r])
        return got[r].reshape(OWNERS * 2, D)

    def emit(value, out, kind, l):
        @pl.when(jnp.logical_and(diag, x == l))
        def _():
            pltpu.make_async_copy(value, out, sem_o.at[kind]).start()

        @pl.when(jnp.logical_and(diag, x != l))
        def _():
            remote(value, out, sem_o_send.at[kind, l], sem_o.at[kind], (l, q)).start()

    wait_for(meta_here, sem_rel.at[4])
    def placed(targets):
        row_of = lax.broadcasted_iota(jnp.int32, (ROWS, 2 * OWNERS), 0)
        slot_of = lax.broadcasted_iota(jnp.int32, (ROWS, 2 * OWNERS), 1)
        hot = jnp.where(row_of.astype(F32) == targets, 1.0, 0.0).astype(BF)
        order = jnp.where(row_of == lax.rem(slot_of, 2) * OWNERS + slot_of // 2, 1.0, 0.0)
        return mm(hot, order.astype(BF))

    at_rows = placed(meta_here[0:1, :])
    pick_t[...] = at_rows.astype(BF)
    pick[...] = turned(at_rows).astype(BF)
    wait_for(xs.at[0], sem_rel.at[0])

    def build_adjacency():
        wait_for(near_here, sem_rel.at[1])
        wait_for(far_here, sem_rel.at[2])

        def entry(row, lane):
            return meta_here[row : row + 1, lane : lane + 1]

        near_lists = [(entry(2, i), entry(3, i)) for i in range(4)]
        far_lists = [(entry(4 + i, 0), entry(4 + i, 1)) for i in range(2)]
        for lists, live, shift, values, target, target_t in (
            (near_lists, entry(6, 0), 0, near_here, adj, adj_t),
            (far_lists, entry(6, 1), 2, far_here, halo, halo_t),
        ):
            tiles = [values[i * BLK : (i + 1) * BLK, :].astype(F32) for i in range(len(lists))]
            for rb in range(2):
                for cb in range(2):
                    total = jnp.zeros((BLK, BLK), F32)
                    for i, (row, col) in enumerate(lists):
                        hit = jnp.logical_and(
                            jnp.logical_and(row == float(rb), col == float(cb + shift)),
                            live > float(i),
                        )
                        total = total + tiles[i] * jnp.where(hit, 1.0, 0.0)
                    target[rb * BLK : (rb + 1) * BLK, cb * BLK : (cb + 1) * BLK] = total.astype(BF)
                    target_t[cb * BLK : (cb + 1) * BLK, rb * BLK : (rb + 1) * BLK] = (
                        total.T.astype(BF)
                    )

    def gain_of(l):
        return meta_all[l, 7:8, :]

    def norm_of(total):
        inv = lax.rsqrt(jnp.mean(total * total, axis=-1, keepdims=True) + EPS)
        return inv, total * inv

    def inner_of(v):
        return jnp.tanh(COEF * (v + CUBIC * v * v * v))

    def slope_of(v, inner):
        return 0.5 * (1.0 + inner) + 0.5 * v * (1.0 - inner * inner) * COEF * (
            1.0 + 3.0 * CUBIC * v * v
        )

    for l in range(LAYERS):
        send_all(l, pick, xs[l])
        if l == 0:
            relocate(cot, gs.at[LAYERS], 64, 3)
            share_weights()
            build_adjacency()
            wait_for(meta_all, sem_m)
        if l == 1:
            pick_home_t[...] = placed(meta[0:1, :]).astype(BF)
        if l == 2:
            send_all(2 * LAYERS, pick, acts[0])
        if l > 0:
            emit(xs.at[l], out_x, 0, l - 1)
            v = normed[l - 1] * gain_of(l - 1)
            slopes[l - 1] = slope_of(v, inner_of(v))
        wait_for(ws.at[l], sem_w.at[l])
        if l == LAYERS - 1:
            wait_for(gs.at[LAYERS], sem_rel.at[3])
            upgrad[...] = mm_nt(gs[LAYERS], ws[l])
        own = mm(adj[...], xs[l])
        total = own + mm(halo[...], receive(l))
        inv, nh = norm_of(total)
        v = nh * gain_of(l)
        inner = inner_of(v)
        inverse[l] = jnp.broadcast_to(inv, (ROWS, BLK))
        normed[l] = nh
        acts[l] = (0.5 * v * (1.0 + inner)).astype(BF)
        if l < LAYERS - 1:
            xs[l + 1] = (xs[l].astype(F32) + mm(acts[l], ws[l])).astype(BF)
        else:
            slopes[l] = slope_of(v, inner)

    def tiles_out(l, partial):
        partial = partial.astype(BF)
        for i in range(32):
            rt, ct = i // 2, i % 2
            wg_out[l, i] = partial[16 * rt : 16 * rt + 16, BLK * ct : BLK * ct + BLK]
        here = x * 8 + wv

        def to_x(i, carry):
            xx = (x + 3 - i) % 4
            for dw in range(8):
                ww = (wv + dw) % 8
                there = xx * 8 + ww
                if dw == 0:

                    @pl.when(there == here)
                    def _():
                        pltpu.make_async_copy(
                            wg_out.at[l, there], wg_in.at[l, here], sem_a.at[l]
                        ).start()

                    @pl.when(there != here)
                    def _():
                        remote(
                            wg_out.at[l, there],
                            wg_in.at[l, here],
                            sem_a_send.at[l],
                            sem_a.at[l],
                            dev(xx, zl, ww),
                        ).start()
                else:
                    remote(
                        wg_out.at[l, there],
                        wg_in.at[l, here],
                        sem_a_send.at[l],
                        sem_a.at[l],
                        dev(xx, zl, ww),
                    ).start()
            return carry

        lax.fori_loop(0, 4, to_x, 0)

    def tiles_z(l):
        wait_for(wg_in.at[l], sem_a.at[l])
        total = wg_in[l, 0].astype(F32)
        for i in range(1, 32):
            total = total + wg_in[l, i].astype(F32)
        zb_out[l] = total
        for dz in (3, 2, 1):
            remote(
                zb_out.at[l],
                zb_in.at[l, zl],
                sem_b_send.at[l],
                sem_b.at[l],
                dev(x, (zl + dz) % 4, wv),
            ).start()
        pltpu.make_async_copy(zb_out.at[l], zb_in.at[l, zl], sem_b.at[l]).start()

    def tiles_home(l):
        wait_for(zb_in.at[l], sem_b.at[l])
        wc_out[l] = (zb_in[l, 0] + zb_in[l, 1] + zb_in[l, 2] + zb_in[l, 3]) * SCALE
        place = out_w.at[
            pl.ds(pl.multiple_of(16 * (4 * x + wv // 2), 16), 16),
            pl.ds(pl.multiple_of(BLK * (wv % 2), BLK), BLK),
        ]
        for dw in (4, 5, 3, 2, 6, 7, 1, 0):
            ww = (wv + dw) % 8
            if dw == 0:

                @pl.when(x == l)
                def _():
                    pltpu.make_async_copy(wc_out.at[l], place, sem_c).start()

                @pl.when(x != l)
                def _():
                    remote(wc_out.at[l], place, sem_c_send.at[l], sem_c, dev(l, zl, ww)).start()
            else:
                remote(wc_out.at[l], place, sem_c_send.at[l], sem_c, dev(l, zl, ww)).start()

    def gains_out(l):
        place = gg_in.at[(4 * x + zl) * 8 + wv]
        for i, dy, dc in in_order:
            cell = base_of[i] + lane_of[dy, dc]
            if (i, dy, dc) == (3, 0, 0):

                @pl.when(x == l)
                def _():
                    pltpu.make_async_copy(gg_out.at[l], place, sem_gg).start()

                @pl.when(x != l)
                def _():
                    remote(gg_out.at[l], place, sem_gg_send.at[l], sem_gg, (l, cell)).start()
            else:
                remote(gg_out.at[l], place, sem_gg_send.at[l], sem_gg, (l, cell)).start()

    def send_home(r, source):
        rows = mm(halo_t[pl.ds(pl.multiple_of(64 * blk, 64), 64), :], source)
        sent[r, pl.ds(32 * blk, 32)] = rows.astype(BF).reshape(32, 2, D)
        for i, dy, dc in in_order:
            cell = base_of[i] + lane_of[dy, dc]
            v = 32 * blk + 8 * z_by_distance[i] + lane_of[dy, dc]
            message = sent.at[r, v]
            if (i, dy, dc) == (3, 0, 0):

                @pl.when(x == 0)
                def _():
                    pltpu.make_async_copy(message, got.at[r, me], sem_got.at[r]).start()

                @pl.when(x != 0)
                def _():
                    remote(
                        message, got.at[r, me], sem_send.at[r], sem_got.at[r], (0, cell)
                    ).start()
            else:
                remote(message, got.at[r, me], sem_send.at[r], sem_got.at[r], (0, cell)).start()

    for l in reversed(range(LAYERS)):
        r = 2 * LAYERS - 1 - l
        if l < LAYERS - 1:
            upgrad[...] = mm_nt(gs[l + 1], ws[l])
        nh = normed[l]
        m = upgrad[...] * slopes[l]
        s = m * gain_of(l)
        t = jnp.mean(s * nh, axis=-1, keepdims=True)
        down = (inverse[l][:, 0:1] * (s - nh * t)).astype(BF)
        if l > 0:
            send_all(r, halo_t, down)
        else:
            send_home(r, down)
        own = mm(adj_t[...], down)
        if l == 0:
            base = gs[1].astype(F32) + own

            @pl.when(jnp.logical_and(diag, x == 0))
            def _():
                base_in[...] = base

            @pl.when(jnp.logical_and(diag, x != 0))
            def _():
                base_out[...] = base
                remote(base_out, base_in, sem_base_send, sem_base, (0, q)).start()

        gg_out[l] = jnp.sum(m * nh, axis=0, keepdims=True)
        gains_out(l)
        if l == 0:
            tiles_z(0)
            tiles_z(1)
        if l == 1:
            near_part = (gs[2].astype(F32) + own).astype(BF)
            far_part = sent[r].reshape(2 * OWNERS, D)
            tiles_out(
                0, mm_tn(acts[0], near_part) + mm_tn(receive(2 * LAYERS), far_part)
            )
        if l > 0:
            tiles_out(l, mm_tn(acts[l], gs[l + 1]))
        if l == LAYERS - 1:
            xs[LAYERS] = (xs[l].astype(F32) + mm(acts[l], ws[l])).astype(BF)
            emit(xs.at[LAYERS], out_x, 0, l)
        else:
            emit(gs.at[l + 1], out_g, 1, l + 1)
        if l in (1, 2):
            tiles_z(l + 1)
        if l in (0, 1):
            tiles_home(l + 2)
        if l > 0:
            gs[l] = (gs[l + 1].astype(F32) + own + mm(pick_t[...], receive(r))).astype(BF)

    tiles_home(0)
    tiles_home(1)

    @pl.when(x == 0)
    def _():
        @pl.when(not_diag)
        def _():
            wait_for(base_in, sem_base)

        spread = mm(pick_home_t[...], receive(2 * LAYERS - 1))
        gs[0] = (base_in[...] + spread).astype(BF)
        pltpu.make_async_copy(gs.at[0], out_g, sem_o.at[1]).start()

    wait_for(gg_in, sem_gg)
    out_gg[...] = jnp.sum(gg_in[...], axis=0) * SCALE

    wait_for(out_x, sem_o.at[0])
    wait_for(out_g, sem_o.at[1])
    wait_for(out_w, sem_c)
    relocated(feats, 64, 0)
    relocated(near, 128, 1)
    relocated(far, 64, 2)
    relocated(cot, 64, 3)

    @pl.when(diag)
    def _():
        wait_for(meta_all.at[pl.ds(0, 3)], sem_rel_send.at[4])

    wait_for(meta_all.at[pl.ds(0, 3)], sem_m_send)
    wait_for(ws.at[pl.ds(0, 3)], sem_w_send)
    for r in range(2 * LAYERS + 1):
        if r != 2 * LAYERS - 1:
            wait_for(sent.at[r, pl.ds(0, OWNERS - 1)], sem_send.at[r])

    @pl.when(x == 0)
    def _():
        wait_for(sent.at[0, pl.ds(0, 31)], sem_send.at[2 * LAYERS - 1])

    @pl.when(x != 0)
    def _():
        wait_for(sent.at[0, pl.ds(0, 32)], sem_send.at[2 * LAYERS - 1])

    @pl.when(jnp.logical_and(diag, x != 0))
    def _():
        wait_for(base_out, sem_base_send)

    for l in range(LAYERS):
        wait_for(wg_in.at[l, pl.ds(0, 31)], sem_a_send.at[l])
        wait_for(zb_in.at[l, pl.ds(0, 3)], sem_b_send.at[l])

        @pl.when(x == l)
        def _():
            wait_for(filler.at[pl.ds(0, 7)], sem_c_send.at[l])
            wait_for(gg_in.at[pl.ds(0, 31)], sem_gg_send.at[l])

        @pl.when(x != l)
        def _():
            wait_for(filler, sem_c_send.at[l])
            wait_for(gg_in.at[pl.ds(0, 32)], sem_gg_send.at[l])

        @pl.when(jnp.logical_and(diag, x != l))
        def _():
            wait_for(gs.at[l], sem_o_send.at[0, l])
            if l > 0:
                wait_for(gs.at[l], sem_o_send.at[1, l])


def settle(*refs):
    ins = [pltpu.make_async_copy(refs[i], refs[8 + i], refs[12].at[i]) for i in range(4)]
    outs = [pltpu.make_async_copy(refs[8 + i], refs[4 + i], refs[13].at[i]) for i in range(4)]
    for copy in ins:
        copy.start()
    for copy, then in zip(ins, outs):
        copy.wait()
        then.start()
    for copy in outs:
        copy.wait()


def on_device(
    feats,
    weights,
    gains,
    send_rows,
    send_count,
    local_index,
    halo_index,
    block_count,
    local_vals,
    halo_vals,
    cotangent,
):
    hbm_spec = pl.BlockSpec(memory_space=pltpu.HBM)
    any_spec = pl.BlockSpec(memory_space=pl.ANY)
    vmem_spec = pl.BlockSpec(memory_space=pltpu.VMEM)
    dma = pltpu.SemaphoreType.DMA
    out_x, out_g, out_w, out_gg = pl.pallas_call(
        kernel,
        out_shape=(
            jax.ShapeDtypeStruct((ROWS, D), BF),
            jax.ShapeDtypeStruct((ROWS, D), BF),
            jax.ShapeDtypeStruct((D, D), F32),
            jax.ShapeDtypeStruct((1, D), F32),
        ),
        in_specs=[hbm_spec] * 11,
        out_specs=(any_spec, any_spec, any_spec, vmem_spec),
        scratch_shapes=[
            pltpu.VMEM((LAYERS + 1, ROWS, D), BF),
            pltpu.VMEM((LAYERS + 1, ROWS, D), BF),
            pltpu.VMEM((LAYERS, D, D), BF),
            pltpu.VMEM((4 * BLK, BLK), BF),
            pltpu.VMEM((2 * BLK, BLK), BF),
            pltpu.VMEM((2, OWNERS), jnp.int32),
            pltpu.VMEM((1, OWNERS), jnp.int32),
            pltpu.VMEM((2, 4), jnp.int32),
            pltpu.VMEM((2, 2), jnp.int32),
            pltpu.VMEM((1, 2), jnp.int32),
            pltpu.VMEM((1, D), F32),
            pltpu.VMEM((8, D), F32),
            pltpu.VMEM((8, D), F32),
            pltpu.VMEM((LAYERS, 8, D), F32),
            pltpu.VMEM((2 * OWNERS, ROWS), BF),
            pltpu.VMEM((ROWS, 2 * OWNERS), BF),
            pltpu.VMEM((ROWS, 2 * OWNERS), BF),
            pltpu.VMEM((ROWS, ROWS), BF),
            pltpu.VMEM((ROWS, ROWS), BF),
            pltpu.VMEM((ROWS, 2 * OWNERS), BF),
            pltpu.VMEM((2 * OWNERS, ROWS), BF),
            pltpu.VMEM((2 * LAYERS + 1, OWNERS, 2, D), BF),
            pltpu.VMEM((2 * LAYERS + 1, OWNERS, 2, D), BF),
            pltpu.VMEM((LAYERS, ROWS, D), F32),
            pltpu.VMEM((LAYERS, ROWS, D), F32),
            pltpu.VMEM((LAYERS, ROWS, BLK), F32),
            pltpu.VMEM((LAYERS, ROWS, D), BF),
            pltpu.VMEM((ROWS, D), F32),
            pltpu.VMEM((LAYERS, 32, 16, BLK), BF),
            pltpu.VMEM((LAYERS, 32, 16, BLK), BF),
            pltpu.VMEM((LAYERS, 16, BLK), F32),
            pltpu.VMEM((LAYERS, 4, 16, BLK), F32),
            pltpu.VMEM((LAYERS, 16, BLK), F32),
            pltpu.VMEM((LAYERS, 1, D), F32),
            pltpu.VMEM((OWNERS, 1, D), F32),
            pltpu.VMEM((ROWS, D), F32),
            pltpu.VMEM((ROWS, D), F32),
            pltpu.VMEM((8, 16, BLK), F32),
            dma((6,)),
            dma((5,)),
            dma((5,)),
            dma,
            dma((LAYERS,)),
            dma,
            dma,
            dma((2 * LAYERS + 1,)),
            dma((2 * LAYERS + 1,)),
            dma((LAYERS,)),
            dma((LAYERS,)),
            dma((LAYERS,)),
            dma((LAYERS,)),
            dma((LAYERS,)),
            dma,
            dma((LAYERS,)),
            dma,
            dma,
            dma,
            dma((2, LAYERS)),
            dma((2,)),
        ],
        compiler_params=pltpu.CompilerParams(
            collective_id=0, has_side_effects=True, vmem_limit_bytes=64 * 1024 * 1024
        ),
    )(
        feats[0],
        weights[0],
        local_vals.reshape(4 * BLK, BLK),
        halo_vals.reshape(2 * BLK, BLK),
        cotangent[0],
        send_rows[0, 0].T,
        send_count[0],
        local_index[0, 0].T,
        halo_index[0, 0],
        block_count[0],
        gains,
    )
    results = (out_x, out_g, out_w, out_gg)
    out_x, out_g, out_w, out_gg = pl.pallas_call(
        settle,
        out_shape=tuple(jax.ShapeDtypeStruct(a.shape, a.dtype) for a in results),
        in_specs=[hbm_spec] * 4,
        out_specs=(hbm_spec,) * 4,
        scratch_shapes=[pltpu.VMEM(a.shape, a.dtype) for a in results] + [dma((4,)), dma((4,))],
        compiler_params=pltpu.CompilerParams(vmem_limit_bytes=64 * 1024 * 1024),
    )(*results)
    return out_x[None, None], out_g[None, None], out_w[None], out_gg


def solution(mesh):
    in_specs = (
        P(None, "cells", None),
        P("segment", None, None),
        P("segment", None),
        P(None, "cells", None, None),
        P(None, "cells", None),
        P(None, "cells", None, None),
        P(None, "cells", None, None),
        P(None, "cells", None),
        P(None, "cells", None, None),
        P(None, "cells", None, None),
        P(None, "cells", None),
    )
    out_specs = (
        P("segment", None, "cells", None),
        P("segment", None, "cells", None),
        P("segment", None, None),
        P("segment", None),
    )
    return jax.shard_map(
        on_device, mesh=mesh, in_specs=in_specs, out_specs=out_specs, check_vma=False
    )
```

```python
import functools
import math

import jax
import jax.numpy as jnp
from jax import lax
from jax.experimental import pallas as pl
from jax.experimental.pallas import tpu as pltpu
from jax.sharding import PartitionSpec as P

EPS = 1e-05
COEF = 0.7978845608028654
CUBIC = 0.044715
LAYERS = 4
D = 256
ROWS = 256
OWNERS = 128
BLK = 128
BF = jnp.bfloat16
F32 = jnp.float32
MESH = pl.DeviceIdType.MESH
SCALE = 1.0 / math.sqrt(OWNERS * ROWS)


def mm(a, b):
    return jnp.dot(a, b, preferred_element_type=F32)


def mm_nt(a, b):
    return lax.dot_general(a, b, (((1,), (1,)), ((), ())), preferred_element_type=F32)


def mm_tn(a, b):
    return lax.dot_general(a, b, (((0,), (0,)), ((), ())), preferred_element_type=F32)


def turned(tile):
    rows = []
    for i in range(2):
        rows.append(
            jnp.concatenate(
                [tile[j * BLK : (j + 1) * BLK, i * BLK : (i + 1) * BLK].T for j in range(2)], axis=1
            )
        )
    return jnp.concatenate(rows, axis=0)


def kernel(
    feats,
    weight,
    near,
    far,
    cot,
    rows_in,
    count_in,
    near_in,
    far_in,
    live_in,
    gains_in,
    out_x,
    out_g,
    out_w,
    out_gg,
    xs,
    gs,
    ws,
    near_here,
    far_here,
    rows_v,
    count_v,
    near_v,
    far_v,
    live_v,
    gains_v,
    meta,
    meta_here,
    meta_all,
    pick,
    pick_t,
    pick_home_t,
    adj,
    adj_t,
    halo,
    halo_t,
    sent,
    got,
    normed,
    slopes,
    inverse,
    acts,
    upgrad,
    wg_out,
    wg_in,
    zb_out,
    zb_in,
    wc_out,
    gg_out,
    gg_in,
    ggz_out,
    ggz_in,
    base_out,
    base_in,
    filler,
    sem_in,
    sem_rel_send,
    sem_rel,
    sem_w_send,
    sem_w,
    sem_m_send,
    sem_m,
    sem_send,
    sem_got,
    sem_a_send,
    sem_a,
    sem_b_send,
    sem_b,
    sem_c_send,
    sem_c,
    sem_gg_send,
    sem_gg,
    sem_ggz_send,
    sem_ggz,
    sem_base_send,
    sem_base,
    sem_o_send,
    sem_o,
):
    x = lax.axis_index("segment")
    q = lax.axis_index("cells")
    z = q // 8
    wv = q % 8
    y = wv // 2
    core = wv % 2
    blk = z // 4
    zl = z % 4

    def seat(xx, zz):
        aside = jnp.where(lax.rem(blk + 4 - xx, 4) == 2, 1, 0)
        return zz + aside * (1 - 2 * lax.rem(zz, 2))

    zo = seat(x, zl)
    me = (4 * x + zo) * 8 + wv
    diag = x == blk
    not_diag = x != blk

    def dev(xx, zz, ww):
        return (xx, (4 * blk + zz) * 8 + ww)

    def remote(src, dst, send, recv, device):
        return pltpu.make_async_remote_copy(
            src, dst, send, recv, device_id=device, device_id_type=MESH
        )

    def wait_for(ref, sem):
        pltpu.make_async_copy(ref, ref, sem).wait()

    small = [
        pltpu.make_async_copy(there, here, sem_in.at[i])
        for i, (there, here) in enumerate(
            (
                (rows_in, rows_v),
                (count_in, count_v),
                (near_in, near_v),
                (far_in, far_v),
                (live_in, live_v),
                (gains_in, gains_v),
            )
        )
    ]
    for copy in small:
        copy.start()

    seg_of = [lax.rem(x + i, 4) for i in range(4)]
    upper = zl // 2
    z_near = zl + 1 - 2 * lax.rem(zl, 2)
    z_by_distance = (3 - 3 * upper, 2 - upper, z_near, zl)
    base_of = [(4 * blk + zz) * 8 for zz in z_by_distance]
    lane_of = {
        (dy, dc): lax.rem(y + dy, 4) * 2 + (lax.rem(core + 1, 2) if dc else core)
        for dy in range(4)
        for dc in range(2)
    }
    seat_of = [
        [32 * seg_of[dx] + 8 * seat(seg_of[dx], z_by_distance[i]) for i in range(4)]
        for dx in range(4)
    ]
    everywhere = sorted(
        (
            (dx, i, dy, dc)
            for dx in range(4)
            for i in range(4)
            for dy in range(4)
            for dc in range(2)
        ),
        key=lambda t: -(
            (0, 1, 2, 1)[t[0]] + (2.5, 1.5, 1.0, 0.0)[t[1]] + (0, 1, 2, 1)[t[2]] + 0.1 * t[3]
        ),
    )
    in_order = sorted(
        ((i, dy, dc) for i in range(4) for dy in range(4) for dc in range(2)),
        key=lambda t: -((2.5, 1.5, 1.0, 0.0)[t[0]] + (0, 1, 2, 1)[t[1]] + 0.1 * t[2]),
    )

    barrier = pltpu.get_barrier_semaphore()

    @pl.when(not_diag)
    def _():
        for xx in range(4):
            pl.semaphore_signal(
                barrier, inc=1, device_id=(xx, (4 * x + zo) * 8 + wv), device_id_type=MESH
            )

    for dx, i, dy, dc in everywhere:
        if (dx, i, dy, dc) != (0, 3, 0, 0):
            pl.semaphore_signal(
                barrier,
                inc=1,
                device_id=(seg_of[dx], base_of[i] + lane_of[dy, dc]),
                device_id_type=MESH,
            )

    for copy in small:
        copy.wait()
    meta[...] = jnp.zeros_like(meta)
    for k in range(2):
        wanted = jnp.where(count_v[...] > k, rows_v[k : k + 1, :], -1)
        meta[0:1, k * OWNERS : (k + 1) * OWNERS] = wanted.astype(F32)
    meta[2:4, 0:4] = near_v[...].astype(F32)
    meta[4:6, 0:2] = far_v[...].astype(F32)
    meta[6:7, 0:2] = live_v[...].astype(F32)
    meta[7:8, :] = gains_v[...]
    pl.semaphore_wait(barrier, 130)

    def relocate(src, dst, rows, k):
        part = src.at[pl.ds(rows * x, rows)]
        there = dst.at[pl.ds(rows * x, rows)]
        for bb in range(4):
            there_z = jnp.where(lax.rem(bb + 4 - blk, 4) == 2, z_near, zl)

            @pl.when(jnp.logical_and(diag, blk == bb))
            def _():
                pltpu.make_async_copy(part, there, sem_rel.at[k]).start()

            @pl.when(jnp.logical_not(jnp.logical_and(diag, blk == bb)))
            def _():
                remote(
                    part,
                    there,
                    sem_rel_send.at[k],
                    sem_rel.at[k],
                    (blk, (4 * bb + there_z) * 8 + wv),
                ).start()

    def relocated(src, rows, k):
        @pl.when(diag)
        def _():
            wait_for(src.at[pl.ds(0, 3 * rows)], sem_rel_send.at[k])

        @pl.when(not_diag)
        def _():
            wait_for(src.at[pl.ds(0, 4 * rows)], sem_rel_send.at[k])

    @pl.when(diag)
    def _():
        for bb in range(4):
            there_z = jnp.where(lax.rem(bb + 4 - blk, 4) == 2, z_near, zl)

            @pl.when(blk == bb)
            def _():
                pltpu.make_async_copy(meta, meta_here, sem_rel.at[4]).start()

            @pl.when(blk != bb)
            def _():
                remote(
                    meta,
                    meta_here,
                    sem_rel_send.at[4],
                    sem_rel.at[4],
                    (blk, (4 * bb + there_z) * 8 + wv),
                ).start()

    relocate(feats, xs.at[0], 64, 0)
    relocate(near, near_here, 128, 1)
    relocate(far, far_here, 64, 2)
    for dx in (2, 1, 3):
        remote(meta, meta_all.at[x], sem_m_send, sem_m, ((x + dx) % 4, q)).start()
    pltpu.make_async_copy(meta, meta_all.at[x], sem_m).start()

    def share_weights():
        for l in range(LAYERS):

            @pl.when(x == l)
            def _():
                for dx in (2, 1, 3):
                    remote(
                        weight, ws.at[l], sem_w_send, sem_w.at[l], ((x + dx) % 4, q)
                    ).start()
                pltpu.make_async_copy(weight, ws.at[l], sem_w.at[l]).start()

    def send_all(r, matrix, source):
        sent[r] = mm(matrix[...], source).astype(BF).reshape(OWNERS, 2, D)
        for dx, i, dy, dc in everywhere:
            v = seat_of[dx][i] + lane_of[dy, dc]
            if (dx, i, dy, dc) == (0, 3, 0, 0):
                pltpu.make_async_copy(sent.at[r, v], got.at[r, v], sem_got.at[r]).start()
            else:
                remote(
                    sent.at[r, v],
                    got.at[r, me],
                    sem_send.at[r],
                    sem_got.at[r],
                    (seg_of[dx], base_of[i] + lane_of[dy, dc]),
                ).start()

    def receive(r):
        wait_for(got.at[r], sem_got.at[r])
        return got[r].reshape(OWNERS * 2, D)

    def emit(value, out, kind, l):
        @pl.when(jnp.logical_and(diag, x == l))
        def _():
            pltpu.make_async_copy(value, out, sem_o.at[kind]).start()

        @pl.when(jnp.logical_and(diag, x != l))
        def _():
            remote(value, out, sem_o_send.at[kind, l], sem_o.at[kind], (l, q)).start()

    wait_for(meta_here, sem_rel.at[4])
    def placed(targets):
        row_of = lax.broadcasted_iota(jnp.int32, (ROWS, 2 * OWNERS), 0)
        slot_of = lax.broadcasted_iota(jnp.int32, (ROWS, 2 * OWNERS), 1)
        hot = jnp.where(row_of.astype(F32) == targets, 1.0, 0.0).astype(BF)
        order = jnp.where(row_of == lax.rem(slot_of, 2) * OWNERS + slot_of // 2, 1.0, 0.0)
        return mm(hot, order.astype(BF))

    at_rows = placed(meta_here[0:1, :])
    pick_t[...] = at_rows.astype(BF)
    pick[...] = turned(at_rows).astype(BF)
    wait_for(xs.at[0], sem_rel.at[0])

    def build_adjacency():
        wait_for(near_here, sem_rel.at[1])
        wait_for(far_here, sem_rel.at[2])

        def entry(row, lane):
            return meta_here[row : row + 1, lane : lane + 1]

        near_lists = [(entry(2, i), entry(3, i)) for i in range(4)]
        far_lists = [(entry(4 + i, 0), entry(4 + i, 1)) for i in range(2)]
        for lists, live, shift, values, target, target_t in (
            (near_lists, entry(6, 0), 0, near_here, adj, adj_t),
            (far_lists, entry(6, 1), 2, far_here, halo, halo_t),
        ):
            tiles = [values[i * BLK : (i + 1) * BLK, :].astype(F32) for i in range(len(lists))]
            for rb in range(2):
                for cb in range(2):
                    total = jnp.zeros((BLK, BLK), F32)
                    for i, (row, col) in enumerate(lists):
                        hit = jnp.logical_and(
                            jnp.logical_and(row == float(rb), col == float(cb + shift)),
                            live > float(i),
                        )
                        total = total + tiles[i] * jnp.where(hit, 1.0, 0.0)
                    target[rb * BLK : (rb + 1) * BLK, cb * BLK : (cb + 1) * BLK] = total.astype(BF)
                    target_t[cb * BLK : (cb + 1) * BLK, rb * BLK : (rb + 1) * BLK] = (
                        total.T.astype(BF)
                    )

    def gain_of(l):
        return meta_all[l, 7:8, :]

    def norm_of(total):
        inv = lax.rsqrt(jnp.mean(total * total, axis=-1, keepdims=True) + EPS)
        return inv, total * inv

    def inner_of(v):
        return jnp.tanh(COEF * (v + CUBIC * v * v * v))

    def slope_of(v, inner):
        return 0.5 * (1.0 + inner) + 0.5 * v * (1.0 - inner * inner) * COEF * (
            1.0 + 3.0 * CUBIC * v * v
        )

    for l in range(LAYERS):
        send_all(l, pick, xs[l])
        if l == 0:
            relocate(cot, gs.at[LAYERS], 64, 3)
            share_weights()
            build_adjacency()
            wait_for(meta_all, sem_m)
        if l == 1:
            pick_home_t[...] = placed(meta[0:1, :]).astype(BF)
        if l == 2:
            send_all(2 * LAYERS, pick, acts[0])
        if l > 0:
            emit(xs.at[l], out_x, 0, l - 1)
            v = normed[l - 1] * gain_of(l - 1)
            slopes[l - 1] = slope_of(v, inner_of(v))
        wait_for(ws.at[l], sem_w.at[l])
        if l == LAYERS - 1:
            wait_for(gs.at[LAYERS], sem_rel.at[3])
            upgrad[...] = mm_nt(gs[LAYERS], ws[l])
        own = mm(adj[...], xs[l])
        total = own + mm(halo[...], receive(l))
        inv, nh = norm_of(total)
        v = nh * gain_of(l)
        inner = inner_of(v)
        inverse[l] = jnp.broadcast_to(inv, (ROWS, BLK))
        normed[l] = nh
        acts[l] = (0.5 * v * (1.0 + inner)).astype(BF)
        if l < LAYERS - 1:
            xs[l + 1] = (xs[l].astype(F32) + mm(acts[l], ws[l])).astype(BF)
        else:
            slopes[l] = slope_of(v, inner)

    def tiles_out(l, partial):
        partial = partial.astype(BF)
        for i in range(32):
            rt, ct = i // 2, i % 2
            wg_out[l, i] = partial[16 * rt : 16 * rt + 16, BLK * ct : BLK * ct + BLK]
        here = x * 8 + wv

        def to_x(i, carry):
            xx = (x + 3 - i) % 4
            for dw in range(8):
                ww = (wv + dw) % 8
                there = xx * 8 + ww
                if dw == 0:

                    @pl.when(there == here)
                    def _():
                        pltpu.make_async_copy(
                            wg_out.at[l, there], wg_in.at[l, here], sem_a.at[l]
                        ).start()

                    @pl.when(there != here)
                    def _():
                        remote(
                            wg_out.at[l, there],
                            wg_in.at[l, here],
                            sem_a_send.at[l],
                            sem_a.at[l],
                            dev(xx, zl, ww),
                        ).start()
                else:
                    remote(
                        wg_out.at[l, there],
                        wg_in.at[l, here],
                        sem_a_send.at[l],
                        sem_a.at[l],
                        dev(xx, zl, ww),
                    ).start()
            return carry

        lax.fori_loop(0, 4, to_x, 0)

    def tiles_z(l):
        wait_for(wg_in.at[l], sem_a.at[l])
        total = wg_in[l, 0].astype(F32)
        for i in range(1, 32):
            total = total + wg_in[l, i].astype(F32)
        zb_out[l] = total
        for dz in (3, 2, 1):
            remote(
                zb_out.at[l],
                zb_in.at[l, zl],
                sem_b_send.at[l],
                sem_b.at[l],
                dev(x, (zl + dz) % 4, wv),
            ).start()
        pltpu.make_async_copy(zb_out.at[l], zb_in.at[l, zl], sem_b.at[l]).start()

    def tiles_home(l):
        wait_for(zb_in.at[l], sem_b.at[l])
        wc_out[l] = (zb_in[l, 0] + zb_in[l, 1] + zb_in[l, 2] + zb_in[l, 3]) * SCALE
        place = out_w.at[
            pl.ds(pl.multiple_of(16 * (4 * x + wv // 2), 16), 16),
            pl.ds(pl.multiple_of(BLK * (wv % 2), BLK), BLK),
        ]
        for dw in (4, 5, 3, 2, 6, 7, 1, 0):
            ww = (wv + dw) % 8
            if dw == 0:

                @pl.when(x == l)
                def _():
                    pltpu.make_async_copy(wc_out.at[l], place, sem_c).start()

                @pl.when(x != l)
                def _():
                    remote(wc_out.at[l], place, sem_c_send.at[l], sem_c, dev(l, zl, ww)).start()
            else:
                remote(wc_out.at[l], place, sem_c_send.at[l], sem_c, dev(l, zl, ww)).start()

    def gains_out(l):
        place = gg_in.at[8 * x + wv] if l > 0 else gg_in.at[(4 * x + zl) * 8 + wv]
        for i, dy, dc in in_order:
            if l > 0 and i < 3:
                continue
            cell = base_of[i] + lane_of[dy, dc]
            if (i, dy, dc) == (3, 0, 0):

                @pl.when(x == l)
                def _():
                    pltpu.make_async_copy(gg_out.at[l], place, sem_gg).start()

                @pl.when(x != l)
                def _():
                    remote(gg_out.at[l], place, sem_gg_send.at[l], sem_gg, (l, cell)).start()
            else:
                remote(gg_out.at[l], place, sem_gg_send.at[l], sem_gg, (l, cell)).start()

    def send_home(r, source):
        rows = mm(halo_t[pl.ds(pl.multiple_of(64 * blk, 64), 64), :], source)
        sent[r, pl.ds(32 * blk, 32)] = rows.astype(BF).reshape(32, 2, D)
        for i, dy, dc in in_order:
            cell = base_of[i] + lane_of[dy, dc]
            v = 32 * blk + 8 * z_by_distance[i] + lane_of[dy, dc]
            message = sent.at[r, v]
            if (i, dy, dc) == (3, 0, 0):

                @pl.when(x == 0)
                def _():
                    pltpu.make_async_copy(message, got.at[r, me], sem_got.at[r]).start()

                @pl.when(x != 0)
                def _():
                    remote(
                        message, got.at[r, me], sem_send.at[r], sem_got.at[r], (0, cell)
                    ).start()
            else:
                remote(message, got.at[r, me], sem_send.at[r], sem_got.at[r], (0, cell)).start()

    for l in reversed(range(LAYERS)):
        r = 2 * LAYERS - 1 - l
        if l < LAYERS - 1:
            upgrad[...] = mm_nt(gs[l + 1], ws[l])
        nh = normed[l]
        m = upgrad[...] * slopes[l]
        s = m * gain_of(l)
        t = jnp.mean(s * nh, axis=-1, keepdims=True)
        down = (inverse[l][:, 0:1] * (s - nh * t)).astype(BF)
        if l > 0:
            send_all(r, halo_t, down)
        else:
            send_home(r, down)
        own = mm(adj_t[...], down)
        if l == 0:
            base = gs[1].astype(F32) + own

            @pl.when(jnp.logical_and(diag, x == 0))
            def _():
                base_in[...] = base

            @pl.when(jnp.logical_and(diag, x != 0))
            def _():
                base_out[...] = base
                remote(base_out, base_in, sem_base_send, sem_base, (0, q)).start()

        gg_out[l] = jnp.sum(m * nh, axis=0, keepdims=True)
        gains_out(l)
        if l == 0:
            tiles_z(0)
            tiles_z(1)
        if l == 1:
            near_part = (gs[2].astype(F32) + own).astype(BF)
            far_part = sent[r].reshape(2 * OWNERS, D)
            tiles_out(
                0, mm_tn(acts[0], near_part) + mm_tn(receive(2 * LAYERS), far_part)
            )
        if l > 0:
            tiles_out(l, mm_tn(acts[l], gs[l + 1]))
        if l == LAYERS - 1:
            xs[LAYERS] = (xs[l].astype(F32) + mm(acts[l], ws[l])).astype(BF)
            emit(xs.at[LAYERS], out_x, 0, l)
        else:
            emit(gs.at[l + 1], out_g, 1, l + 1)
        if l in (1, 2):
            tiles_z(l + 1)
        if l in (0, 1):
            tiles_home(l + 2)
        if l == 0:
            tiles_home(0)
        if l > 0:
            gs[l] = (gs[l + 1].astype(F32) + own + mm(pick_t[...], receive(r))).astype(BF)

    tiles_home(1)

    @pl.when(x == 0)
    def _():
        @pl.when(not_diag)
        def _():
            wait_for(base_in, sem_base)

        spread = mm(pick_home_t[...], receive(2 * LAYERS - 1))
        gs[0] = (base_in[...] + spread).astype(BF)
        pltpu.make_async_copy(gs.at[0], out_g, sem_o.at[1]).start()

    @pl.when(x == 0)
    def _():
        wait_for(gg_in, sem_gg)
        out_gg[...] = jnp.sum(gg_in[...], axis=0) * SCALE

    @pl.when(x != 0)
    def _():
        wait_for(gg_in.at[pl.ds(0, 32)], sem_gg)
        ggz_out[...] = jnp.sum(gg_in[0:32], axis=0)
        for i in range(3):
            remote(ggz_out, ggz_in.at[zl], sem_ggz_send, sem_ggz, (x, base_of[i] + wv)).start()
        pltpu.make_async_copy(ggz_out, ggz_in.at[zl], sem_ggz).start()
        wait_for(ggz_in, sem_ggz)
        out_gg[...] = jnp.sum(ggz_in[...], axis=0) * SCALE
        wait_for(ggz_in.at[pl.ds(0, 3)], sem_ggz_send)


    wait_for(out_x, sem_o.at[0])
    wait_for(out_g, sem_o.at[1])
    wait_for(out_w, sem_c)
    relocated(feats, 64, 0)
    relocated(near, 128, 1)
    relocated(far, 64, 2)
    relocated(cot, 64, 3)

    @pl.when(diag)
    def _():
        wait_for(meta_all.at[pl.ds(0, 3)], sem_rel_send.at[4])

    wait_for(meta_all.at[pl.ds(0, 3)], sem_m_send)
    wait_for(ws.at[pl.ds(0, 3)], sem_w_send)
    for r in range(2 * LAYERS + 1):
        if r != 2 * LAYERS - 1:
            wait_for(sent.at[r, pl.ds(0, OWNERS - 1)], sem_send.at[r])

    @pl.when(x == 0)
    def _():
        wait_for(sent.at[0, pl.ds(0, 31)], sem_send.at[2 * LAYERS - 1])

    @pl.when(x != 0)
    def _():
        wait_for(sent.at[0, pl.ds(0, 32)], sem_send.at[2 * LAYERS - 1])

    @pl.when(jnp.logical_and(diag, x != 0))
    def _():
        wait_for(base_out, sem_base_send)

    for l in range(LAYERS):
        wait_for(wg_in.at[l, pl.ds(0, 31)], sem_a_send.at[l])
        wait_for(zb_in.at[l, pl.ds(0, 3)], sem_b_send.at[l])

        @pl.when(x == l)
        def _():
            wait_for(filler.at[pl.ds(0, 7)], sem_c_send.at[l])
            wait_for(gg_in.at[pl.ds(0, 7 if l else 31)], sem_gg_send.at[l])

        @pl.when(x != l)
        def _():
            wait_for(filler, sem_c_send.at[l])
            wait_for(gg_in.at[pl.ds(0, 8 if l else 32)], sem_gg_send.at[l])

        @pl.when(jnp.logical_and(diag, x != l))
        def _():
            wait_for(gs.at[l], sem_o_send.at[0, l])
            if l > 0:
                wait_for(gs.at[l], sem_o_send.at[1, l])


def settle(*refs):
    ins = [pltpu.make_async_copy(refs[i], refs[8 + i], refs[12].at[i]) for i in range(4)]
    outs = [pltpu.make_async_copy(refs[8 + i], refs[4 + i], refs[13].at[i]) for i in range(4)]
    for copy in ins:
        copy.start()
    for copy, then in zip(ins, outs):
        copy.wait()
        then.start()
    for copy in outs:
        copy.wait()


def on_device(
    feats,
    weights,
    gains,
    send_rows,
    send_count,
    local_index,
    halo_index,
    block_count,
    local_vals,
    halo_vals,
    cotangent,
):
    hbm_spec = pl.BlockSpec(memory_space=pltpu.HBM)
    any_spec = pl.BlockSpec(memory_space=pl.ANY)
    vmem_spec = pl.BlockSpec(memory_space=pltpu.VMEM)
    dma = pltpu.SemaphoreType.DMA
    out_x, out_g, out_w, out_gg = pl.pallas_call(
        kernel,
        out_shape=(
            jax.ShapeDtypeStruct((ROWS, D), BF),
            jax.ShapeDtypeStruct((ROWS, D), BF),
            jax.ShapeDtypeStruct((D, D), F32),
            jax.ShapeDtypeStruct((1, D), F32),
        ),
        in_specs=[hbm_spec] * 11,
        out_specs=(any_spec, any_spec, any_spec, vmem_spec),
        scratch_shapes=[
            pltpu.VMEM((LAYERS + 1, ROWS, D), BF),
            pltpu.VMEM((LAYERS + 1, ROWS, D), BF),
            pltpu.VMEM((LAYERS, D, D), BF),
            pltpu.VMEM((4 * BLK, BLK), BF),
            pltpu.VMEM((2 * BLK, BLK), BF),
            pltpu.VMEM((2, OWNERS), jnp.int32),
            pltpu.VMEM((1, OWNERS), jnp.int32),
            pltpu.VMEM((2, 4), jnp.int32),
            pltpu.VMEM((2, 2), jnp.int32),
            pltpu.VMEM((1, 2), jnp.int32),
            pltpu.VMEM((1, D), F32),
            pltpu.VMEM((8, D), F32),
            pltpu.VMEM((8, D), F32),
            pltpu.VMEM((LAYERS, 8, D), F32),
            pltpu.VMEM((2 * OWNERS, ROWS), BF),
            pltpu.VMEM((ROWS, 2 * OWNERS), BF),
            pltpu.VMEM((ROWS, 2 * OWNERS), BF),
            pltpu.VMEM((ROWS, ROWS), BF),
            pltpu.VMEM((ROWS, ROWS), BF),
            pltpu.VMEM((ROWS, 2 * OWNERS), BF),
            pltpu.VMEM((2 * OWNERS, ROWS), BF),
            pltpu.VMEM((2 * LAYERS + 1, OWNERS, 2, D), BF),
            pltpu.VMEM((2 * LAYERS + 1, OWNERS, 2, D), BF),
            pltpu.VMEM((LAYERS, ROWS, D), F32),
            pltpu.VMEM((LAYERS, ROWS, D), F32),
            pltpu.VMEM((LAYERS, ROWS, BLK), F32),
            pltpu.VMEM((LAYERS, ROWS, D), BF),
            pltpu.VMEM((ROWS, D), F32),
            pltpu.VMEM((LAYERS, 32, 16, BLK), BF),
            pltpu.VMEM((LAYERS, 32, 16, BLK), BF),
            pltpu.VMEM((LAYERS, 16, BLK), F32),
            pltpu.VMEM((LAYERS, 4, 16, BLK), F32),
            pltpu.VMEM((LAYERS, 16, BLK), F32),
            pltpu.VMEM((LAYERS, 1, D), F32),
            pltpu.VMEM((OWNERS, 1, D), F32),
            pltpu.VMEM((1, D), F32),
            pltpu.VMEM((4, 1, D), F32),
            pltpu.VMEM((ROWS, D), F32),
            pltpu.VMEM((ROWS, D), F32),
            pltpu.VMEM((8, 16, BLK), F32),
            dma((6,)),
            dma((5,)),
            dma((5,)),
            dma,
            dma((LAYERS,)),
            dma,
            dma,
            dma((2 * LAYERS + 1,)),
            dma((2 * LAYERS + 1,)),
            dma((LAYERS,)),
            dma((LAYERS,)),
            dma((LAYERS,)),
            dma((LAYERS,)),
            dma((LAYERS,)),
            dma,
            dma((LAYERS,)),
            dma,
            dma,
            dma,
            dma,
            dma,
            dma((2, LAYERS)),
            dma((2,)),
        ],
        compiler_params=pltpu.CompilerParams(
            collective_id=0, has_side_effects=True, vmem_limit_bytes=64 * 1024 * 1024
        ),
    )(
        feats[0],
        weights[0],
        local_vals.reshape(4 * BLK, BLK),
        halo_vals.reshape(2 * BLK, BLK),
        cotangent[0],
        send_rows[0, 0].T,
        send_count[0],
        local_index[0, 0].T,
        halo_index[0, 0],
        block_count[0],
        gains,
    )
    results = (out_x, out_g, out_w, out_gg)
    out_x, out_g, out_w, out_gg = pl.pallas_call(
        settle,
        out_shape=tuple(jax.ShapeDtypeStruct(a.shape, a.dtype) for a in results),
        in_specs=[hbm_spec] * 4,
        out_specs=(hbm_spec,) * 4,
        scratch_shapes=[pltpu.VMEM(a.shape, a.dtype) for a in results] + [dma((4,)), dma((4,))],
        compiler_params=pltpu.CompilerParams(vmem_limit_bytes=64 * 1024 * 1024),
    )(*results)
    return out_x[None, None], out_g[None, None], out_w[None], out_gg


def solution(mesh):
    in_specs = (
        P(None, "cells", None),
        P("segment", None, None),
        P("segment", None),
        P(None, "cells", None, None),
        P(None, "cells", None),
        P(None, "cells", None, None),
        P(None, "cells", None, None),
        P(None, "cells", None),
        P(None, "cells", None, None),
        P(None, "cells", None, None),
        P(None, "cells", None),
    )
    out_specs = (
        P("segment", None, "cells", None),
        P("segment", None, "cells", None),
        P("segment", None, None),
        P("segment", None),
    )
    return jax.shard_map(
        on_device, mesh=mesh, in_specs=in_specs, out_specs=out_specs, check_vma=False
    )
```
